32 devices in a mesh: grp: 2 (over y), doc: 8 (over z, x), layer: 2 (over core).
Axes of the slice: x: 2, y: 2, z: 4, core: 2. Of those that a mesh axis runs over, the one named last changes fastest.
Arguments:
- query_grads: bfloat16 [2048, 2, 4096], P(('grp', 'doc'), 'layer'), parts along dimension 0, may hold values from -6 to 6
- doc_grads: bfloat16 [6144, 2, 4096], P(('grp', 'doc'), 'layer'), parts along dimension 0, may hold values from -0.0625 to 0.0625
- query_ids: int32 [2048], P('grp'), parts along dimension 0, may hold values from 0 to 3071
- doc_ids: int32 [6144], P(('grp', 'doc')), parts along dimension 0, may hold values from 0 to 3071, each once
Outputs:
- scores: float32 [2048, 3072], P('grp', ('doc', 'layer')), parts along dimension 0
The draws below stay inside these ranges and needn't reach their ends.
There are 2 independent parts, one for each index of `grp`. The reference program is written for one: setup_inputs(seed, part) draws one part's arguments, and reference() takes and returns one part's arrays. A program takes and returns all parts, laid end to end along the dimension named above; each array names one. Nothing has to cross between parts.
Inputs may be any that keep to these rules, and one draw needn't show every extreme that they name: doc_ids names every document number once.
All inputs are finite; a program needn't handle non-finite values.
Results may differ from the reference program's by a relative error of at most 0.0003.
Values may be sent and summed in bfloat16 or wider, within the bound.
A program may use at most 64 MiB of HBM per device.

```python
import jax
import jax.numpy as jnp
from jax import lax

K = 4096
QUERIES = 1024
LAYERS = 2
DOCS = 3072


def touch_ends(drawn, own_key, smallest, largest):
    longest = drawn.shape.index(max(drawn.shape))
    spots = []
    for shift in (0, 1):
        where = [jax.random.randint(jax.random.fold_in(own_key, axis), (), 0, length) for axis, length in enumerate(drawn.shape)]
        where[longest] = (where[longest] + shift) % drawn.shape[longest]
        spots.append(tuple(where))
    return drawn.at[spots[0]].set(smallest).at[spots[1]].set(largest)


def levels(stream_key, shape, shards, low, largest):
    def one(position, blocks):
        draws = jax.random.uniform(jax.random.fold_in(jax.random.fold_in(stream_key, 6), position), (blocks,), jnp.float32, low / len(shards), largest / len(shards))
        return jnp.repeat(jnp.exp(draws), shape[position] // blocks).reshape((-1,) + (1,) * (len(shape) - position - 1))

    loudness = one(*shards[0])
    for cut in shards[1:]:
        loudness = loudness * one(*cut)
    return loudness


def noise(stream_key, shape, spread, limit, shards=(), held_as=jnp.bfloat16):
    result = jax.random.normal(stream_key, shape, jnp.float32) * spread
    if len(shards) > 0:
        result = levels(stream_key, shape, shards, -0.22, 0.18) * result
    return jnp.clip(result, min=-limit, max=limit).astype(held_as)


def setup_inputs(seed: int = 0, part: int = 0) -> dict:
    seeds = jax.random.split(jax.random.key(seed), 5)
    part_keys = jax.random.split(jax.random.fold_in(seeds[4], part), 5)
    return {
        "query_grads": noise(part_keys[0], (QUERIES, LAYERS, K), 1.0, 6.0, ((0, 8), (1, 2))),
        "doc_grads": noise(part_keys[1], (DOCS, LAYERS, K), (LAYERS * K) ** -0.5, 0.0625, ((0, 8), (1, 2))),
        "query_ids": touch_ends(jax.random.randint(part_keys[2], (QUERIES,), 0, DOCS), jax.random.fold_in(part_keys[2], 1), 0, DOCS - 1).astype(jnp.int32),
        "doc_ids": jax.random.permutation(part_keys[3], DOCS).astype(jnp.int32),
    }


def reference(query_grads, doc_grads, query_ids, doc_ids):
    queries = query_grads.reshape(QUERIES, LAYERS * K)
    documents = doc_grads.reshape(DOCS, LAYERS * K)
    raw = lax.dot_general(queries, documents, (((1,), (1,)), ((), ())), preferred_element_type=jnp.float32)
    same = query_ids[:, None] == doc_ids[None, :]
    return jnp.where(same, jnp.zeros_like(raw), raw)
```

```python
import functools

import jax
import jax.numpy as jnp
from jax import lax
from jax.experimental import pallas as pl
from jax.experimental.pallas import tpu as pltpu
from jax.sharding import PartitionSpec as P

MESH = pl.DeviceIdType.MESH
NT = (((1,), (1,)), ((), ()))


def kernel(
    nz, q_ref, d_ref, o_ref, Q, D, CS, CR, ACC, XR,
    loc, xq_s, xq_r, xd_s, xd_r, up_s, up_r, dn_s, dn_r, c_s, c_r, o_s, o_r,
):
    g, d, c = lax.axis_index("grp"), lax.axis_index("doc"), lax.axis_index("layer")
    z, x = d // 2, d % 2
    partner, other = (g, d + 1 - 2 * x, c), (g, d, 1 - c)
    above, below = (g, d + 2, c), (g, d - 2, c)
    has_above, has_below = z < nz - 1, z > 0
    rows, half = Q.shape[2], Q.shape[3]
    ch = rows // 2
    nd = D.shape[1] // 2
    dch = D.shape[1] // xd_s.shape[0]
    mine = pl.multiple_of(x * half, half)
    theirs = pl.multiple_of((1 - x) * half, half)

    barrier = pltpu.get_barrier_semaphore()

    def greet(device):
        pl.semaphore_signal(barrier, inc=1, device_id=device, device_id_type=MESH)

    greet(partner)
    greet(other)

    @pl.when(has_above)
    def _():
        greet(above)

    @pl.when(has_below)
    def _():
        greet(below)

    own_q = pltpu.make_async_copy(q_ref.at[:, pl.ds(mine, half)], Q.at[z, 0], loc.at[0])
    own_d = pltpu.make_async_copy(d_ref.at[:, pl.ds(mine, half)], D.at[0], loc.at[1])
    own_q.start()
    own_d.start()
    pl.semaphore_wait(barrier, 2 + jnp.where(has_above, 1, 0) + jnp.where(has_below, 1, 0))

    def remote(src, dst, ss, rs, device):
        return pltpu.make_async_remote_copy(
            src_ref=src, dst_ref=dst, send_sem=ss, recv_sem=rs, device_id=device, device_id_type=MESH
        )

    def xq(h):
        r = pl.ds(h * ch, ch)
        return remote(q_ref.at[r, pl.ds(theirs, half)], Q.at[z, 1, r], xq_s.at[h], xq_r.at[h], partner)

    def xd(k):
        r = pl.ds(k * dch, dch)
        return remote(d_ref.at[r, pl.ds(theirs, half)], D.at[1, r], xd_s.at[k], xd_r.at[k], partner)

    def chunk(zq, sub):
        return Q.at[zq, sub // 2, pl.ds(pl.multiple_of(sub % 2 * ch, ch), ch)]

    def going_up(i):
        at = chunk(z - i // 4, i % 4)
        return remote(at, at, up_s.at[i], up_r.at[i], above)

    def going_down(i):
        at = chunk(z + i // 4, i % 4)
        return remote(at, at, dn_s.at[i], dn_r.at[i], below)

    def from_below(i):
        at = chunk(z - 1 - i // 4, i % 4)
        return remote(at, at, up_s.at[i], up_r.at[i], above)

    def from_above(i):
        at = chunk(z + 1 + i // 4, i % 4)
        return remote(at, at, dn_s.at[i], dn_r.at[i], below)

    def send_both(i):
        @pl.when(has_above)
        def _():
            going_up(i).start()

        @pl.when(has_below)
        def _():
            going_down(i).start()

    for h in range(2):
        xq(h).start()
    own_q.wait()
    for h in range(2):
        send_both(h)
    for h in range(2):
        xq(h).wait_recv()
        send_both(2 + h)
    for k in range(xd_s.shape[0]):
        xd(k).start()

    n_above, n_below = 4 * (nz - 1 - z), 4 * z

    def relay(j, _):
        @pl.when(j < n_above)
        def _():
            from_above(j).wait_recv()

            @pl.when(has_below)
            def _():
                going_down(j + 4).start()

        @pl.when(j < n_below)
        def _():
            from_below(j).wait_recv()

            @pl.when(has_above)
            def _():
                going_up(j + 4).start()

        return 0

    lax.fori_loop(0, 4 * (nz - 2), relay, 0)
    own_d.wait()
    for k in range(xd_s.shape[0]):
        xd(k).wait_recv()

    def core(t):
        return remote(CS.at[t], CR.at[t], c_s.at[t], c_r.at[t], other)

    def out(t):
        swapped = t + 1 - 2 * (t % 2)
        return remote(ACC.at[t, 1], XR.at[swapped], o_s.at[t], o_r.at[swapped], partner)

    def arrived(t):
        return remote(ACC.at[t, 1], XR.at[t], o_s.at[t], o_r.at[t], partner)

    def z_of(t):
        return jnp.where(z < nz // 2, t // 2, nz - 1 - t // 2)

    def multiply(t):
        queries = Q[z_of(t), t % 2]
        for core_half, into in ((1 - c, CS), (c, ACC)):
            lines = pl.ds(pl.multiple_of(core_half * nd, nd), nd)
            for who in (1, 0):
                into[t, who] = lax.dot_general(
                    D[who, lines, :], queries, NT, preferred_element_type=jnp.float32
                )
            if into is CS:
                core(t).start()

    def hand_over(t):
        core(t).wait_recv()
        ACC[t, 1] = ACC[t, 1] + CR[t, 1]
        out(t).start()
        ACC[t, 0] = ACC[t, 0] + CR[t, 0]

    def step(t, _):
        @pl.when((t >= 2 * nz - 2) & (z == 0))
        def _():
            for h in range(2):
                from_above(2 * t - 4 + h).wait_recv()

        @pl.when((t >= 2 * nz - 2) & (z == nz - 1))
        def _():
            for h in range(2):
                from_below(2 * t - 4 + h).wait_recv()

        multiply(t)

        @pl.when(t > 0)
        def _():
            hand_over(t - 1)

        return 0

    lax.fori_loop(0, 2 * nz, step, 0)
    hand_over(2 * nz - 1)

    def finish(t, _):
        arrived(t).wait_recv()
        origin = jnp.where(t % 2 == 0, x, 1 - x)
        at = pl.multiple_of((z_of(t) * 2 + origin) * rows, rows)
        o_ref[:, pl.ds(at, rows)] = ACC[t, 0] + XR[t]
        return 0

    lax.fori_loop(0, 2 * nz, finish, 0)

    for h in range(2):
        xq(h).wait_send()
    for k in range(xd_s.shape[0]):
        xd(k).wait_send()

    def drain(t, _):
        core(t).wait_send()
        out(t).wait_send()
        return 0

    lax.fori_loop(0, 2 * nz, drain, 0)

    @pl.when(has_above)
    def _():
        lax.fori_loop(0, 4 * (z + 1), lambda i, _: (going_up(i).wait_send(), 0)[1], 0)

    @pl.when(has_below)
    def _():
        lax.fori_loop(0, 4 * (nz - z), lambda i, _: (going_down(i).wait_send(), 0)[1], 0)


def exchange(queries, documents, n):
    rows, k = queries.shape
    nd = documents.shape[0] // 2
    nz, half, dc = n // 2, k // 2, 4
    steps = 2 * nz
    block = (nd, rows)
    dma = pltpu.SemaphoreType.DMA
    return pl.pallas_call(
        functools.partial(kernel, nz),
        out_shape=jax.ShapeDtypeStruct((nd, n * rows), jnp.float32),
        in_specs=[pl.BlockSpec(memory_space=pl.ANY)] * 2,
        out_specs=pl.BlockSpec(memory_space=pltpu.VMEM),
        scratch_shapes=[
            pltpu.VMEM((nz, 2, rows, half), jnp.bfloat16),
            pltpu.VMEM((2, 2 * nd, half), jnp.bfloat16),
            pltpu.VMEM((steps, 2) + block, jnp.float32),
            pltpu.VMEM((steps, 2) + block, jnp.float32),
            pltpu.VMEM((steps, 2) + block, jnp.float32),
            pltpu.VMEM((steps,) + block, jnp.float32),
            dma((2,)),
            dma((2,)), dma((2,)), dma((dc,)), dma((dc,)),
            dma((4 * nz,)), dma((4 * nz,)), dma((4 * nz,)), dma((4 * nz,)),
            dma((steps,)), dma((steps,)), dma((steps,)), dma((steps,)),
        ],
        compiler_params=pltpu.CompilerParams(
            collective_id=0, has_side_effects=True, vmem_limit_bytes=48 * 2**20
        ),
        cost_estimate=pl.CostEstimate(
            flops=4 * n * rows * nd * k, bytes_accessed=32 * 2**20, transcendentals=0
        ),
    )(queries, documents)


def on_device(n, query_grads, doc_grads, query_ids, doc_ids):
    queries = query_grads.reshape(query_grads.shape[0], -1)
    documents = doc_grads.reshape(doc_grads.shape[0], -1)
    rows, nd = queries.shape[0], documents.shape[0] // 2
    if rows % 128 or nd % 16 or n % 2 or n < 4 or n * rows > 1024 or queries.shape[1] % 256:
        every = lax.all_gather(queries, "doc", axis=0, tiled=True)
        raw = lax.dot_general(every, documents, NT, preferred_element_type=jnp.float32)
        same = query_ids[:, None] == doc_ids[None, :]
        partial_scores = jnp.where(same, jnp.zeros_like(raw), raw)
        return lax.psum_scatter(partial_scores, "layer", scatter_dimension=1, tiled=True)
    raw = exchange(queries, documents, n)
    ids = lax.dynamic_slice(doc_ids, (lax.axis_index("layer") * nd,), (nd,))
    return jnp.where(ids[:, None] == query_ids[None, :], jnp.zeros_like(raw), raw).T


def solution(mesh):
    in_specs = (
        P(("grp", "doc"), "layer", None),
        P(("grp", "doc"), "layer", None),
        P("grp"),
        P(("grp", "doc")),
    )
    out_specs = P("grp", ("doc", "layer"))
    return jax.shard_map(
        functools.partial(on_device, mesh.shape["doc"]),
        mesh=mesh, in_specs=in_specs, out_specs=out_specs, check_vma=False,
    )
```

```python
import functools
import math

import jax
import jax.numpy as jnp
from jax import lax
from jax.experimental import pallas as pl
from jax.experimental.pallas import tpu as pltpu
from jax.sharding import PartitionSpec as P

MESH = pl.DeviceIdType.MESH
NT = (((1,), (1,)), ((), ()))
STEP = math.log(2) / 128
TOP = 32700.0


def encode(into, sums):
    n = sums.shape[0]
    peak = jnp.maximum(jnp.max(jnp.abs(sums), axis=0, keepdims=True), 1e-30)
    level = jnp.ceil(jnp.log(peak) / STEP) + 1
    units = jnp.round(sums * (jnp.exp(level * -STEP) * TOP))
    into[pl.ds(0, n)] = units.astype(jnp.int32).astype(jnp.int16)
    level = jnp.broadcast_to(level.astype(jnp.int32), (16, sums.shape[1]))
    into[pl.ds(n, 16)] = level.astype(jnp.int16)


def decode(coded):
    n = coded.shape[0] - 16
    level = coded[pl.ds(n, 16)].astype(jnp.int32).astype(jnp.float32)[:1]
    units = coded[pl.ds(0, n)].astype(jnp.int32).astype(jnp.float32)
    return units * (jnp.exp(level * STEP) / TOP)


def kernel(
    nz, q_ref, d_ref, o_ref, QA, QB, DA, DB, HA, CS, CR, ACC, XS, XR, HCS, HCR, HACC, HS, RET,
    loc, xq_s, xq_r, xd_s, xd_r, up_s, up_r, dn_s, dn_r, h_s, h_r, c_s, c_r, o_s, o_r, hc_s, hc_r, ret_s, ret_r,
):
    g, d, c = lax.axis_index("grp"), lax.axis_index("doc"), lax.axis_index("layer")
    z, x = d // 2, d % 2
    partner, other = (g, d + 1 - 2 * x, c), (g, d, 1 - c)
    above, below = (g, d + 2, c), (g, d - 2, c)
    has_above, has_below = z < nz - 1, z > 0
    is_end = (z == 0) | (z == nz - 1)
    is_helper = (z == 1) | (z == nz - 2)
    helper = (g, jnp.where(z == 0, d + 2, d - 2), c)
    helped = (g, jnp.where(z == 1, d - 2, d + 2), c)
    rows, ka, kb = QA.shape[2], QA.shape[3], QB.shape[3]
    half = ka + kb
    ch = rows // 2
    nd = DA.shape[1] // 2

    def columns(part, mine):
        start = jnp.where(mine, x, 1 - x) * half + (ka if part else 0)
        return pl.ds(pl.multiple_of(start, 128), kb if part else ka)

    barrier = pltpu.get_barrier_semaphore()

    def greet(device):
        pl.semaphore_signal(barrier, inc=1, device_id=device, device_id_type=MESH)

    greet(partner)
    greet(other)

    @pl.when(has_above)
    def _():
        greet(above)

    @pl.when(has_below)
    def _():
        greet(below)

    def own(part):
        Q, D = (QA, QB)[part], (DA, DB)[part]
        return (
            pltpu.make_async_copy(q_ref.at[:, columns(part, True)], Q.at[z, 0], loc.at[part]),
            pltpu.make_async_copy(d_ref.at[:, columns(part, True)], D.at[0], loc.at[2 + part]),
        )

    for kind in (0, 1):
        for part in (0, 1):
            own(part)[kind].start()
    pl.semaphore_wait(barrier, 2 + jnp.where(has_above, 1, 0) + jnp.where(has_below, 1, 0))

    def remote(src, dst, ss, rs, device):
        return pltpu.make_async_remote_copy(
            src_ref=src, dst_ref=dst, send_sem=ss, recv_sem=rs, device_id=device, device_id_type=MESH
        )

    def xq(h, part):
        r = pl.ds(h * ch, ch)
        return remote(
            q_ref.at[r, columns(part, False)], (QA, QB)[part].at[z, 1, r], xq_s.at[h, part], xq_r.at[h, part], partner
        )

    def xd(h, part):
        r = pl.ds(h * nd, nd)
        return remote(
            d_ref.at[r, columns(part, False)], (DA, DB)[part].at[1, r], xd_s.at[h, part], xd_r.at[h, part], partner
        )

    def chunk(part, zq, sub):
        return (QA, QB)[part].at[zq, sub // 2, pl.ds(pl.multiple_of(sub % 2 * ch, ch), ch)]

    def going_up(i, part):
        at = chunk(part, z - i // 4, i % 4)
        return remote(at, at, up_s.at[i, part], up_r.at[i, part], above)

    def going_down(i, part):
        at = chunk(part, z + i // 4, i % 4)
        return remote(at, at, dn_s.at[i, part], dn_r.at[i, part], below)

    def from_below(i, part):
        at = chunk(part, z - 1 - i // 4, i % 4)
        return remote(at, at, up_s.at[i, part], up_r.at[i, part], above)

    def from_above(i, part):
        at = chunk(part, z + 1 + i // 4, i % 4)
        return remote(at, at, dn_s.at[i, part], dn_r.at[i, part], below)

    def both_parts(act, with_b, with_a):
        @pl.when(with_b)
        def _():
            act(1)

        @pl.when(with_a)
        def _():
            act(0)

    def send_up(i):
        both_parts(lambda part: going_up(i, part).start(), has_above, z < nz - 2)

    def send_down(i):
        both_parts(lambda part: going_down(i, part).start(), has_below, z > 1)

    for h in range(2):
        for part in (1, 0):
            xq(h, part).start()
    for part in (0, 1):
        own(part)[0].wait()
    for h in range(2):
        send_up(h)
        send_down(h)
    for h in range(2):
        for part in (1, 0):
            xq(h, part).wait_recv()
        send_up(2 + h)
        send_down(2 + h)
    for part in (0, 1):
        for h in range(2):
            xd(h, part).start()
    for part in (0, 1):
        own(part)[1].wait()

    def lend(who, h):
        at = pl.ds(h * nd, nd)
        return remote(DA.at[who, at], HA.at[who, at], h_s.at[who, h], h_r.at[who, h], helper)

    @pl.when(is_end)
    def _():
        for h in range(2):
            lend(0, h).start()
        for h in range(2):
            xd(h, 0).wait_recv()
            lend(1, h).start()

    n_above, n_below = 4 * (nz - 1 - z), 4 * z

    def relay(j, _):
        @pl.when(j < n_above)
        def _():
            both_parts(lambda part: from_above(j, part).wait_recv(), True, has_below)
            send_down(j + 4)

        @pl.when(j < n_below)
        def _():
            both_parts(lambda part: from_below(j, part).wait_recv(), True, has_above)
            send_up(j + 4)

        return 0

    lax.fori_loop(0, 4 * (nz - 2), relay, 0)

    @pl.when(~is_end)
    def _():
        for h in range(2):
            xd(h, 0).wait_recv()

    for h in range(2):
        xd(h, 1).wait_recv()

    def core(t):
        return remote(CS.at[t], CR.at[t], c_s.at[t], c_r.at[t], other)

    def helper_core(t):
        return remote(HCS.at[t], HCR.at[t], hc_s.at[t], hc_r.at[t], other)

    def give_back(t):
        return remote(HS.at[t], RET.at[t], ret_s.at[t], ret_r.at[t], helped)

    def out(t):
        swapped = t + 1 - 2 * (t % 2)
        return remote(XS.at[t], XR.at[swapped], o_s.at[t], o_r.at[swapped], partner)

    def arrived(t):
        return remote(XS.at[t], XR.at[t], o_s.at[t], o_r.at[t], partner)

    def z_of(o):
        return jnp.where(z < nz // 2, o, nz - 1 - o)

    def product(documents, queries):
        return lax.dot_general(documents, queries, NT, preferred_element_type=jnp.float32)

    def pair(ref, zq):
        return ref[zq].reshape(2 * rows, ref.shape[3])

    def lines(core_half):
        return pl.ds(pl.multiple_of(core_half * nd, nd), nd)

    def multiply(o):
        zq = z_of(o)
        for core_half, into in ((1 - c, CS), (c, ACC)):
            for who in (1, 0):
                part = product(DB[who, lines(core_half), :], pair(QB, zq))
                for s in (0, 1):
                    into[2 * o + s, who] = part[:, s * rows : (s + 1) * rows]

                @pl.when((~is_end) | (o == 0))
                def _():
                    more = product(DA[who, lines(core_half), :], pair(QA, zq))
                    for s in (0, 1):
                        into[2 * o + s, who] = into[2 * o + s, who] + more[:, s * rows : (s + 1) * rows]

            if into is CS:
                for s in (0, 1):
                    core(2 * o + s).start()

    def help_multiply(o):
        zq = jnp.where(z == 1, 1 + o, nz - 2 - o)
        for core_half, into in ((1 - c, HCS), (c, HACC)):
            for who in (1, 0):
                part = product(HA[who, lines(core_half), :], pair(QA, zq))
                for s in (0, 1):
                    into[2 * o + s, who] = part[:, s * rows : (s + 1) * rows]
            if into is HCS:
                for s in (0, 1):
                    helper_core(2 * o + s).start()

    def help_hand_over(o):
        for s in (0, 1):
            t = 2 * o + s
            helper_core(t).wait_recv()
            for who in (1, 0):
                encode(HS.at[t, who], HACC[t, who] + HCR[t, who])
            give_back(t).start()

    def hand_over(o):
        @pl.when(is_end & (o > 0))
        def _():
            for s in (0, 1):
                t = 2 * o + s
                give_back(t - 2).wait_recv()
                for who in (1, 0):
                    ACC[t, who] = ACC[t, who] + decode(RET.at[t - 2, who])

        for s in (0, 1):
            t = 2 * o + s
            core(t).wait_recv()
            encode(XS.at[t], ACC[t, 1] + CR[t, 1])
            out(t).start()
            ACC[t, 0] = ACC[t, 0] + CR[t, 0]

    @pl.when(is_helper)
    def _():
        for who in (0, 1):
            for h in range(2):
                lend(who, h).wait_recv()

    def step(o, _):
        @pl.when((o == nz - 1) & (z == 0))
        def _():
            for h in range(4):
                from_above(4 * (nz - 2) + h, 1).wait_recv()

        @pl.when((o == nz - 1) & (z == nz - 1))
        def _():
            for h in range(4):
                from_below(4 * (nz - 2) + h, 1).wait_recv()

        @pl.when(is_helper & (o < nz - 1))
        def _():
            help_multiply(o)

        multiply(o)

        @pl.when(is_helper & (o < nz - 1))
        def _():
            help_hand_over(o)

        @pl.when(o > 0)
        def _():
            hand_over(o - 1)

        return 0

    lax.fori_loop(0, nz, step, 0)
    hand_over(nz - 1)

    def finish(t, _):
        arrived(t).wait_recv()
        origin = jnp.where(t % 2 == 0, x, 1 - x)
        at = pl.multiple_of((z_of(t // 2) * 2 + origin) * rows, rows)
        o_ref[:, pl.ds(at, rows)] = ACC[t, 0] + decode(XR.at[t])
        return 0

    lax.fori_loop(0, 2 * nz, finish, 0)

    for h in range(2):
        for part in (0, 1):
            xq(h, part).wait_send()
            xd(h, part).wait_send()

    def drain(t, _):
        core(t).wait_send()
        out(t).wait_send()
        return 0

    lax.fori_loop(0, 2 * nz, drain, 0)

    @pl.when(is_end)
    def _():
        for who in (0, 1):
            for h in range(2):
                lend(who, h).wait_send()

    @pl.when(is_helper)
    def _():
        def drain_help(t, _):
            helper_core(t).wait_send()
            give_back(t).wait_send()
            return 0

        lax.fori_loop(0, 2 * nz - 2, drain_help, 0)

    def drain_up(i, _):
        both_parts(lambda part: going_up(i, part).wait_send(), True, z < nz - 2)
        return 0

    def drain_down(i, _):
        both_parts(lambda part: going_down(i, part).wait_send(), True, z > 1)
        return 0

    @pl.when(has_above)
    def _():
        lax.fori_loop(0, 4 * (z + 1), drain_up, 0)

    @pl.when(has_below)
    def _():
        lax.fori_loop(0, 4 * (nz - z), drain_down, 0)


def exchange(queries, documents, n):
    rows, k = queries.shape
    nd = documents.shape[0] // 2
    nz, half = n // 2, k // 2
    ka = half // 128 * 3 // 8 * 128
    kb = half - ka
    steps, helps = 2 * nz, 2 * nz - 2
    block, coded = (nd, rows), (nd + 16, rows)
    dma = pltpu.SemaphoreType.DMA
    return pl.pallas_call(
        functools.partial(kernel, nz),
        out_shape=jax.ShapeDtypeStruct((nd, n * rows), jnp.float32),
        in_specs=[pl.BlockSpec(memory_space=pl.ANY)] * 2,
        out_specs=pl.BlockSpec(memory_space=pltpu.VMEM),
        scratch_shapes=[
            pltpu.VMEM((nz, 2, rows, ka), jnp.bfloat16),
            pltpu.VMEM((nz, 2, rows, kb), jnp.bfloat16),
            pltpu.VMEM((2, 2 * nd, ka), jnp.bfloat16),
            pltpu.VMEM((2, 2 * nd, kb), jnp.bfloat16),
            pltpu.VMEM((2, 2 * nd, ka), jnp.bfloat16),
            pltpu.VMEM((steps, 2) + block, jnp.float32),
            pltpu.VMEM((steps, 2) + block, jnp.float32),
            pltpu.VMEM((steps, 2) + block, jnp.float32),
            pltpu.VMEM((steps,) + coded, jnp.int16),
            pltpu.VMEM((steps,) + coded, jnp.int16),
            pltpu.VMEM((helps, 2) + block, jnp.float32),
            pltpu.VMEM((helps, 2) + block, jnp.float32),
            pltpu.VMEM((helps, 2) + block, jnp.float32),
            pltpu.VMEM((helps, 2) + coded, jnp.int16),
            pltpu.VMEM((helps, 2) + coded, jnp.int16),
            dma((4,)),
            dma((2, 2)), dma((2, 2)), dma((2, 2)), dma((2, 2)),
            dma((4 * nz, 2)), dma((4 * nz, 2)), dma((4 * nz, 2)), dma((4 * nz, 2)),
            dma((2, 2)), dma((2, 2)),
            dma((steps,)), dma((steps,)), dma((steps,)), dma((steps,)),
            dma((helps,)), dma((helps,)), dma((helps,)), dma((helps,)),
        ],
        compiler_params=pltpu.CompilerParams(
            collective_id=0, has_side_effects=True, vmem_limit_bytes=60 * 2**20
        ),
        cost_estimate=pl.CostEstimate(
            flops=4 * n * rows * nd * k, bytes_accessed=32 * 2**20, transcendentals=0
        ),
    )(queries, documents)


def on_device(n, query_grads, doc_grads, query_ids, doc_ids):
    queries = query_grads.reshape(query_grads.shape[0], -1)
    documents = doc_grads.reshape(doc_grads.shape[0], -1)
    rows, nd = queries.shape[0], documents.shape[0] // 2
    if rows % 128 or nd % 16 or n % 2 or n < 8 or n * rows > 1024 or queries.shape[1] % 2048:
        every = lax.all_gather(queries, "doc", axis=0, tiled=True)
        raw = lax.dot_general(every, documents, NT, preferred_element_type=jnp.float32)
        same = query_ids[:, None] == doc_ids[None, :]
        partial_scores = jnp.where(same, jnp.zeros_like(raw), raw)
        return lax.psum_scatter(partial_scores, "layer", scatter_dimension=1, tiled=True)
    raw = exchange(queries, documents, n)
    ids = jnp.where(lax.axis_index("layer") == 0, doc_ids[:nd], doc_ids[nd:])
    return jnp.where(ids[:, None] == query_ids[None, :], jnp.zeros_like(raw), raw).T


def solution(mesh):
    in_specs = (
        P(("grp", "doc"), "layer", None),
        P(("grp", "doc"), "layer", None),
        P("grp"),
        P(("grp", "doc")),
    )
    out_specs = P("grp", ("doc", "layer"))
    return jax.shard_map(
        functools.partial(on_device, mesh.shape["doc"]),
        mesh=mesh, in_specs=in_specs, out_specs=out_specs, check_vma=False,
    )
```

```python
import functools
import math

import jax
import jax.numpy as jnp
from jax import lax
from jax.experimental import pallas as pl
from jax.experimental.pallas import tpu as pltpu
from jax.sharding import PartitionSpec as P

MESH = pl.DeviceIdType.MESH
NT = (((1,), (1,)), ((), ()))
STEP = math.log(2) / 128
TOP = 32700.0


def encode(into, sums):
    n = sums.shape[0]
    peak = jnp.maximum(jnp.max(jnp.abs(sums), axis=0, keepdims=True), 1e-30)
    level = jnp.ceil(jnp.log(peak) / STEP) + 1
    units = jnp.round(sums * (jnp.exp(level * -STEP) * TOP))
    into[pl.ds(0, n)] = units.astype(jnp.int32).astype(jnp.int16)
    level = jnp.broadcast_to(level.astype(jnp.int32), (16, sums.shape[1]))
    into[pl.ds(n, 16)] = level.astype(jnp.int16)


def decode(coded):
    n = coded.shape[0] - 16
    level = coded[pl.ds(n, 16)].astype(jnp.int32).astype(jnp.float32)[:1]
    units = coded[pl.ds(0, n)].astype(jnp.int32).astype(jnp.float32)
    return units * (jnp.exp(level * STEP) / TOP)


def kernel(
    nz, q_ref, d_ref, o_ref, QA, QB, DA, DB, HA, SUM, CR, XS, XR, HSUM, HCR, HS, RET,
    loc, xq_s, xq_r, xd_s, xd_r, up_s, up_r, dn_s, dn_r, h_s, h_r, c_s, c_r, o_s, o_r, hc_s, hc_r, ret_s, ret_r,
):
    g, d, c = lax.axis_index("grp"), lax.axis_index("doc"), lax.axis_index("layer")
    z, x = d // 2, d % 2
    partner, other = (g, d + 1 - 2 * x, c), (g, d, 1 - c)
    above, below = (g, d + 2, c), (g, d - 2, c)
    has_above, has_below = z < nz - 1, z > 0
    is_end = (z == 0) | (z == nz - 1)
    is_helper = (z == 1) | (z == nz - 2)
    helper = (g, jnp.where(z == 0, d + 2, d - 2), c)
    helped = (g, jnp.where(z == 1, d - 2, d + 2), c)
    rows, ka, kb = QA.shape[2], QA.shape[3], QB.shape[3]
    half = ka + kb
    ch = rows // 2
    nd = DA.shape[1] // 2

    def columns(part, mine):
        start = jnp.where(mine, x, 1 - x) * half + (ka if part else 0)
        return pl.ds(pl.multiple_of(start, 128), kb if part else ka)

    barrier = pltpu.get_barrier_semaphore()

    def greet(device):
        pl.semaphore_signal(barrier, inc=1, device_id=device, device_id_type=MESH)

    greet(partner)
    greet(other)

    @pl.when(has_above)
    def _():
        greet(above)

    @pl.when(has_below)
    def _():
        greet(below)

    def own(part):
        Q, D = (QA, QB)[part], (DA, DB)[part]
        return (
            pltpu.make_async_copy(q_ref.at[:, columns(part, True)], Q.at[z, 0], loc.at[part]),
            pltpu.make_async_copy(d_ref.at[:, columns(part, True)], D.at[0], loc.at[2 + part]),
        )

    for part in (0, 1):
        for copy in own(part):
            copy.start()
    pl.semaphore_wait(barrier, 2 + jnp.where(has_above, 1, 0) + jnp.where(has_below, 1, 0))

    def remote(src, dst, ss, rs, device):
        return pltpu.make_async_remote_copy(
            src_ref=src, dst_ref=dst, send_sem=ss, recv_sem=rs, device_id=device, device_id_type=MESH
        )

    def xq(h, part):
        r = pl.ds(h * ch, ch)
        return remote(
            q_ref.at[r, columns(part, False)], (QA, QB)[part].at[z, 1, r], xq_s.at[h, part], xq_r.at[h, part], partner
        )

    def xd(h, part):
        r = pl.ds(h * nd, nd)
        return remote(
            d_ref.at[r, columns(part, False)], (DA, DB)[part].at[1, r], xd_s.at[h, part], xd_r.at[h, part], partner
        )

    def chunk(part, zq, sub):
        return (QA, QB)[part].at[zq, sub // 2, pl.ds(pl.multiple_of(sub % 2 * ch, ch), ch)]

    def going_up(i, part):
        at = chunk(part, z - i // 4, i % 4)
        return remote(at, at, up_s.at[i, part], up_r.at[i, part], above)

    def going_down(i, part):
        at = chunk(part, z + i // 4, i % 4)
        return remote(at, at, dn_s.at[i, part], dn_r.at[i, part], below)

    def from_below(i, part):
        at = chunk(part, z - 1 - i // 4, i % 4)
        return remote(at, at, up_s.at[i, part], up_r.at[i, part], above)

    def from_above(i, part):
        at = chunk(part, z + 1 + i // 4, i % 4)
        return remote(at, at, dn_s.at[i, part], dn_r.at[i, part], below)

    def both_parts(act, with_b, with_a):
        @pl.when(with_b)
        def _():
            act(1)

        @pl.when(with_a)
        def _():
            act(0)

    def send_up(i):
        both_parts(lambda part: going_up(i, part).start(), has_above, z < nz - 2)

    def send_down(i):
        both_parts(lambda part: going_down(i, part).start(), has_below, z > 1)

    for h in range(2):
        for part in (1, 0):
            xq(h, part).start()
    for part in (0, 1):
        own(part)[0].wait()
    for h in range(2):
        send_up(h)
        send_down(h)
    for h in range(2):
        for part in (1, 0):
            xq(h, part).wait_recv()
        send_up(2 + h)
        send_down(2 + h)
    for part in (0, 1):
        for h in range(2):
            xd(h, part).start()
    for part in (0, 1):
        own(part)[1].wait()

    def lend(who, h):
        at = pl.ds(h * nd, nd)
        return remote(DA.at[who, at], HA.at[who, at], h_s.at[who, h], h_r.at[who, h], helper)

    @pl.when(is_end)
    def _():
        for h in range(2):
            xd(h, 0).wait_recv()
            lend(1, h).start()
        for h in range(2):
            lend(0, h).start()

    n_above, n_below = 4 * (nz - 1 - z), 4 * z

    def relay(j, _):
        @pl.when(j < n_above)
        def _():
            both_parts(lambda part: from_above(j, part).wait_recv(), True, has_below)
            send_down(j + 4)

        @pl.when(j < n_below)
        def _():
            both_parts(lambda part: from_below(j, part).wait_recv(), True, has_above)
            send_up(j + 4)

        return 0

    def core(o, who):
        return remote(SUM.at[1, o, who], CR.at[o, who], c_s.at[o, who], c_r.at[o, who], other)

    def helper_core(o, who):
        return remote(HSUM.at[1, o, who], HCR.at[o, who], hc_s.at[o, who], hc_r.at[o, who], other)

    def give_back(o, who):
        return remote(HS.at[o, who], RET.at[o, who], ret_s.at[o, who], ret_r.at[o, who], helped)

    def out(o):
        return remote(XS.at[o], XR.at[o], o_s.at[o], o_r.at[o], partner)

    def z_of(o):
        return jnp.where(z < nz // 2, o, nz - 1 - o)

    def product(documents, queries):
        return lax.dot_general(documents, queries, NT, preferred_element_type=jnp.float32)

    def pair(ref, zq):
        return ref[zq].reshape(2 * rows, ref.shape[3])

    def each(low, high, body):
        lax.fori_loop(low, high, lambda o, _: (body(o), 0)[1], 0)

    def multiply(who, h, low, high):
        lines, slot = pl.ds(h * nd, nd), jnp.where(c == h, 0, 1)

        def body(o):
            zq = z_of(o)
            SUM[slot, o, who] = product(DB[who, lines, :], pair(QB, zq))

            @pl.when((~is_end) | (o == 0))
            def _():
                SUM[slot, o, who] = SUM[slot, o, who] + product(DA[who, lines, :], pair(QA, zq))

            @pl.when(c != h)
            def _():
                core(o, who).start()

        each(low, high, body)

    def add_up(who, h, low, high):
        def body(o):
            core(o, who).wait_recv()
            SUM[0, o, who] = SUM[0, o, who] + CR[o, who]

            @pl.when(is_end & (o > 0))
            def _():
                give_back(o - 1, who).wait_recv()
                SUM[0, o, who] = SUM[0, o, who] + decode(RET.at[o - 1, who])

            if who == 1:
                encode(XS.at[o], SUM[0, o, 1])
                out(o).start()

        @pl.when(c == h)
        def _():
            each(low, high, body)

    def help_multiply(who, h, low, high):
        lines, slot = pl.ds(h * nd, nd), jnp.where(c == h, 0, 1)

        def body(o):
            zq = jnp.where(z == 1, 1 + o, nz - 2 - o)
            HSUM[slot, o, who] = product(HA[who, lines, :], pair(QA, zq))

            @pl.when(c != h)
            def _():
                helper_core(o, who).start()

        each(low, high, body)

    def help_add_up(who, h, low, high):
        def body(o):
            helper_core(o, who).wait_recv()
            encode(HS.at[o, who], HSUM[0, o, who] + HCR[o, who])
            give_back(o, who).start()

        @pl.when(c == h)
        def _():
            each(low, high, body)

    total = 4 * (nz - 2)
    first = jnp.where(is_end, total, total - 2)
    lax.fori_loop(0, first, relay, 0)

    @pl.when(is_helper)
    def _():
        for h in range(2):
            lend(1, h).wait_recv()
            help_multiply(1, h, 0, nz - 2)
        for h in range(2):
            help_add_up(1, h, 0, nz - 2)

    @pl.when(~is_end)
    def _():
        for h in range(2):
            xd(h, 0).wait_recv()

    xd(0, 1).wait_recv()
    multiply(1, 0, 0, nz - 1)
    add_up(1, 0, 0, nz - 1)
    for h in range(2):
        multiply(0, h, 0, nz - 1)

    lax.fori_loop(first, total, relay, 0)

    @pl.when(is_helper)
    def _():
        for h in range(2):
            help_multiply(1, h, nz - 2, nz - 1)
        for h in range(2):
            help_add_up(1, h, nz - 2, nz - 1)
        lend(0, 0).wait_recv()
        help_multiply(0, 0, 0, nz - 1)

    @pl.when(z == 0)
    def _():
        for h in range(4):
            from_above(total + h, 1).wait_recv()

    @pl.when(z == nz - 1)
    def _():
        for h in range(4):
            from_below(total + h, 1).wait_recv()

    multiply(1, 0, nz - 1, nz)
    xd(1, 1).wait_recv()
    multiply(1, 1, 0, nz)

    @pl.when(is_helper)
    def _():
        help_add_up(0, 0, 0, nz - 1)
        lend(0, 1).wait_recv()
        help_multiply(0, 1, 0, nz - 1)

    add_up(1, 0, nz - 1, nz)
    add_up(1, 1, 0, nz)

    @pl.when(is_helper)
    def _():
        help_add_up(0, 1, 0, nz - 1)

    for h in range(2):
        multiply(0, h, nz - 1, nz)
    for h in range(2):
        add_up(0, h, 0, nz)

    def finish(o):
        out(o).wait_recv()
        sums = decode(XR.at[o])
        for s in (0, 1):
            at = pl.multiple_of((z_of(o) * 2 + jnp.where(x == s, 0, 1)) * rows, rows)
            mine, theirs = pl.ds(s * rows, rows), slice((1 - s) * rows, (2 - s) * rows)
            o_ref[:, pl.ds(at, rows)] = SUM[0, o, 0, :, mine] + sums[:, theirs]

    each(0, nz, finish)

    for h in range(2):
        for part in (0, 1):
            xq(h, part).wait_send()
            xd(h, part).wait_send()

    for h in range(2):

        @pl.when(c != h)
        def _():
            each(0, nz, lambda o: [core(o, who).wait_send() for who in (0, 1)])

    each(0, nz, lambda o: out(o).wait_send())

    @pl.when(is_end)
    def _():
        for who in (0, 1):
            for h in range(2):
                lend(who, h).wait_send()

    @pl.when(is_helper)
    def _():
        def drain_help(o):
            for who in (0, 1):
                helper_core(o, who).wait_send()
                give_back(o, who).wait_send()

        each(0, nz - 1, drain_help)

    def drain_up(i, _):
        both_parts(lambda part: going_up(i, part).wait_send(), True, z < nz - 2)
        return 0

    def drain_down(i, _):
        both_parts(lambda part: going_down(i, part).wait_send(), True, z > 1)
        return 0

    @pl.when(has_above)
    def _():
        lax.fori_loop(0, 4 * (z + 1), drain_up, 0)

    @pl.when(has_below)
    def _():
        lax.fori_loop(0, 4 * (nz - z), drain_down, 0)


def exchange(queries, documents, n):
    rows, k = queries.shape
    nd = documents.shape[0] // 2
    nz, half = n // 2, k // 2
    ka = half // 128 * 3 // 8 * 128
    kb = half - ka
    block, coded = (nd, 2 * rows), (nd + 16, 2 * rows)
    dma = pltpu.SemaphoreType.DMA
    return pl.pallas_call(
        functools.partial(kernel, nz),
        out_shape=jax.ShapeDtypeStruct((nd, n * rows), jnp.float32),
        in_specs=[pl.BlockSpec(memory_space=pltpu.HBM)] * 2,
        out_specs=pl.BlockSpec(memory_space=pltpu.VMEM),
        scratch_shapes=[
            pltpu.VMEM((nz, 2, rows, ka), jnp.bfloat16),
            pltpu.VMEM((nz, 2, rows, kb), jnp.bfloat16),
            pltpu.VMEM((2, 2 * nd, ka), jnp.bfloat16),
            pltpu.VMEM((2, 2 * nd, kb), jnp.bfloat16),
            pltpu.VMEM((2, 2 * nd, ka), jnp.bfloat16),
            pltpu.VMEM((2, nz, 2) + block, jnp.float32),
            pltpu.VMEM((nz, 2) + block, jnp.float32),
            pltpu.VMEM((nz,) + coded, jnp.int16),
            pltpu.VMEM((nz,) + coded, jnp.int16),
            pltpu.VMEM((2, nz - 1, 2) + block, jnp.float32),
            pltpu.VMEM((nz - 1, 2) + block, jnp.float32),
            pltpu.VMEM((nz - 1, 2) + coded, jnp.int16),
            pltpu.VMEM((nz - 1, 2) + coded, jnp.int16),
            dma((4,)),
            dma((2, 2)), dma((2, 2)), dma((2, 2)), dma((2, 2)),
            dma((4 * nz, 2)), dma((4 * nz, 2)), dma((4 * nz, 2)), dma((4 * nz, 2)),
            dma((2, 2)), dma((2, 2)),
            dma((nz, 2)), dma((nz, 2)), dma((nz,)), dma((nz,)),
            dma((nz - 1, 2)), dma((nz - 1, 2)), dma((nz - 1, 2)), dma((nz - 1, 2)),
        ],
        compiler_params=pltpu.CompilerParams(
            collective_id=0, has_side_effects=True, vmem_limit_bytes=52 * 2**20
        ),
        cost_estimate=pl.CostEstimate(
            flops=4 * n * rows * nd * k, bytes_accessed=32 * 2**20, transcendentals=0
        ),
    )(queries, documents)


def on_device(n, query_grads, doc_grads, query_ids, doc_ids):
    queries = query_grads.reshape(query_grads.shape[0], -1)
    documents = doc_grads.reshape(doc_grads.shape[0], -1)
    rows, nd = queries.shape[0], documents.shape[0] // 2
    if rows % 128 or nd % 16 or n % 2 or n < 8 or n * rows > 1024 or queries.shape[1] % 2048:
        every = lax.all_gather(queries, "doc", axis=0, tiled=True)
        raw = lax.dot_general(every, documents, NT, preferred_element_type=jnp.float32)
        same = query_ids[:, None] == doc_ids[None, :]
        partial_scores = jnp.where(same, jnp.zeros_like(raw), raw)
        return lax.psum_scatter(partial_scores, "layer", scatter_dimension=1, tiled=True)
    raw = exchange(queries, documents, n)
    ids = jnp.where(lax.axis_index("layer") == 0, doc_ids[:nd], doc_ids[nd:])
    return jnp.where(ids[:, None] == query_ids[None, :], jnp.zeros_like(raw), raw).T


def solution(mesh):
    in_specs = (
        P(("grp", "doc"), "layer", None),
        P(("grp", "doc"), "layer", None),
        P("grp"),
        P(("grp", "doc")),
    )
    out_specs = P("grp", ("doc", "layer"))
    return jax.shard_map(
        functools.partial(on_device, mesh.shape["doc"]),
        mesh=mesh, in_specs=in_specs, out_specs=out_specs, check_vma=False,
    )
```

```python
import functools
import math

import jax
import jax.numpy as jnp
from jax import lax
from jax.experimental import pallas as pl
from jax.experimental.pallas import tpu as pltpu
from jax.sharding import PartitionSpec as P

MESH = pl.DeviceIdType.MESH
NT = (((1,), (1,)), ((), ()))
STEP = math.log(2) / 128
TOP = 32700.0


def encode(into, sums):
    n = sums.shape[0]
    peak = jnp.maximum(jnp.max(jnp.abs(sums), axis=0, keepdims=True), 1e-30)
    level = jnp.ceil(jnp.log(peak) / STEP) + 1
    units = jnp.round(sums * (jnp.exp(level * -STEP) * TOP))
    into[pl.ds(0, n)] = units.astype(jnp.int32).astype(jnp.int16)
    level = jnp.broadcast_to(level.astype(jnp.int32), (16, sums.shape[1]))
    into[pl.ds(n, 16)] = level.astype(jnp.int16)


def decode(coded):
    n = coded.shape[0] - 16
    level = coded[pl.ds(n, 16)].astype(jnp.int32).astype(jnp.float32)[:1]
    units = coded[pl.ds(0, n)].astype(jnp.int32).astype(jnp.float32)
    return units * (jnp.exp(level * STEP) / TOP)


def kernel(
    nz, q_ref, d_ref, o_ref, QA, QB, DA, DB, HA, SUM, CR, XS, XR, HSUM, HCR, HS, RET,
    loc, xq_s, xq_r, xd_s, xd_r, up_s, up_r, dn_s, dn_r, h_s, h_r, c_s, c_r, o_s, o_r, hc_s, hc_r, ret_s, ret_r,
):
    g, d, c = lax.axis_index("grp"), lax.axis_index("doc"), lax.axis_index("layer")
    z, x = d // 2, d % 2
    partner, other = (g, d + 1 - 2 * x, c), (g, d, 1 - c)
    above, below = (g, d + 2, c), (g, d - 2, c)
    has_above, has_below = z < nz - 1, z > 0
    is_end = (z == 0) | (z == nz - 1)
    is_helper = (z == 1) | (z == nz - 2)
    helper = (g, jnp.where(z == 0, d + 2, d - 2), c)
    helped = (g, jnp.where(z == 1, d - 2, d + 2), c)
    rows, ka, kb = QA.shape[2], QA.shape[3], QB.shape[3]
    half = ka + kb
    ch = rows // 2
    nd = DA.shape[1] // 2

    def columns(part, mine):
        start = jnp.where(mine, x, 1 - x) * half + (ka if part else 0)
        return pl.ds(pl.multiple_of(start, 128), kb if part else ka)

    barrier = pltpu.get_barrier_semaphore()

    def greet(device):
        pl.semaphore_signal(barrier, inc=1, device_id=device, device_id_type=MESH)

    greet(partner)
    greet(other)

    @pl.when(has_above)
    def _():
        greet(above)

    @pl.when(has_below)
    def _():
        greet(below)

    def own(part):
        Q, D = (QA, QB)[part], (DA, DB)[part]
        return (
            pltpu.make_async_copy(q_ref.at[:, columns(part, True)], Q.at[z, 0], loc.at[part]),
            pltpu.make_async_copy(d_ref.at[:, columns(part, True)], D.at[0], loc.at[2 + part]),
        )

    for part in (0, 1):
        for copy in own(part):
            copy.start()
    pl.semaphore_wait(barrier, 2 + jnp.where(has_above, 1, 0) + jnp.where(has_below, 1, 0))

    def remote(src, dst, ss, rs, device):
        return pltpu.make_async_remote_copy(
            src_ref=src, dst_ref=dst, send_sem=ss, recv_sem=rs, device_id=device, device_id_type=MESH
        )

    def xq(h, part):
        r = pl.ds(h * ch, ch)
        return remote(
            q_ref.at[r, columns(part, False)], (QA, QB)[part].at[z, 1, r], xq_s.at[h, part], xq_r.at[h, part], partner
        )

    def xd(h, part):
        r = pl.ds(h * nd, nd)
        return remote(
            d_ref.at[r, columns(part, False)], (DA, DB)[part].at[1, r], xd_s.at[h, part], xd_r.at[h, part], partner
        )

    def chunk(part, zq, sub):
        return (QA, QB)[part].at[zq, sub // 2, pl.ds(pl.multiple_of(sub % 2 * ch, ch), ch)]

    def going_up(i, part, first=False):
        at = chunk(part, z - i // 4, i % 4)
        src = q_ref.at[pl.ds(i * ch, ch), columns(part, True)] if first else at
        return remote(src, at, up_s.at[i, part], up_r.at[i, part], above)

    def going_down(i, part, first=False):
        at = chunk(part, z + i // 4, i % 4)
        src = q_ref.at[pl.ds(i * ch, ch), columns(part, True)] if first else at
        return remote(src, at, dn_s.at[i, part], dn_r.at[i, part], below)

    def from_below(i, part):
        at = chunk(part, z - 1 - i // 4, i % 4)
        return remote(at, at, up_s.at[i, part], up_r.at[i, part], above)

    def from_above(i, part):
        at = chunk(part, z + 1 + i // 4, i % 4)
        return remote(at, at, dn_s.at[i, part], dn_r.at[i, part], below)

    def both_parts(act, with_b, with_a):
        @pl.when(with_b)
        def _():
            act(1)

        @pl.when(with_a)
        def _():
            act(0)

    def send_up(i):
        both_parts(lambda part: going_up(i, part).start(), has_above, z < nz - 2)

    def send_down(i):
        both_parts(lambda part: going_down(i, part).start(), has_below, z > 1)

    for h in range(2):
        for part in (1, 0):
            xq(h, part).start()
    for h in range(2):
        both_parts(lambda part: going_up(h, part, True).start(), has_above, z < nz - 2)
        both_parts(lambda part: going_down(h, part, True).start(), has_below, z > 1)
    for h in range(2):
        for part in (1, 0):
            xq(h, part).wait_recv()
        send_up(2 + h)
        send_down(2 + h)
    for part in (0, 1):
        for h in range(2):
            xd(h, part).start()
    for part in (0, 1):
        for copy in own(part):
            copy.wait()

    def lend(who, h):
        at = pl.ds(h * nd, nd)
        return remote(DA.at[who, at], HA.at[who, at], h_s.at[who, h], h_r.at[who, h], helper)

    @pl.when(is_end)
    def _():
        for h in range(2):
            xd(h, 0).wait_recv()
            lend(1, h).start()
        for h in range(2):
            lend(0, h).start()

    n_above, n_below = 4 * (nz - 1 - z), 4 * z

    def relay(j, _):
        @pl.when(j < n_above)
        def _():
            both_parts(lambda part: from_above(j, part).wait_recv(), True, has_below)
            send_down(j + 4)

        @pl.when(j < n_below)
        def _():
            both_parts(lambda part: from_below(j, part).wait_recv(), True, has_above)
            send_up(j + 4)

        return 0

    def core(o, who):
        return remote(SUM.at[1, o, who], CR.at[o, who], c_s.at[o, who], c_r.at[o, who], other)

    def helper_core(o, who):
        return remote(HSUM.at[1, o, who], HCR.at[o, who], hc_s.at[o, who], hc_r.at[o, who], other)

    def give_back(o, who):
        return remote(HS.at[o, who], RET.at[o, who], ret_s.at[o, who], ret_r.at[o, who], helped)

    def out(o):
        return remote(XS.at[o], XR.at[o], o_s.at[o], o_r.at[o], partner)

    def z_of(o):
        return jnp.where(z < nz // 2, o, nz - 1 - o)

    def product(documents, queries):
        return lax.dot_general(documents, queries, NT, preferred_element_type=jnp.float32)

    def pair(ref, zq):
        return ref[zq].reshape(2 * rows, ref.shape[3])

    def each(low, high, body):
        lax.fori_loop(low, high, lambda o, _: (body(o), 0)[1], 0)

    def multiply(who, h, low, high):
        lines, slot = pl.ds(h * nd, nd), jnp.where(c == h, 0, 1)

        def body(o):
            zq = z_of(o)
            SUM[slot, o, who] = product(DB[who, lines, :], pair(QB, zq))

            @pl.when((~is_end) | (o == 0))
            def _():
                SUM[slot, o, who] = SUM[slot, o, who] + product(DA[who, lines, :], pair(QA, zq))

            @pl.when(c != h)
            def _():
                core(o, who).start()

        each(low, high, body)

    def add_up(who, h, low, high):
        def body(o):
            core(o, who).wait_recv()
            SUM[0, o, who] = SUM[0, o, who] + CR[o, who]

            @pl.when(is_end & (o > 0))
            def _():
                give_back(o - 1, who).wait_recv()
                SUM[0, o, who] = SUM[0, o, who] + decode(RET.at[o - 1, who])

            if who == 1:
                encode(XS.at[o], SUM[0, o, 1])
                out(o).start()

        @pl.when(c == h)
        def _():
            each(low, high, body)

    def help_multiply(who, h, low, high):
        lines, slot = pl.ds(h * nd, nd), jnp.where(c == h, 0, 1)

        def body(o):
            zq = jnp.where(z == 1, 1 + o, nz - 2 - o)
            HSUM[slot, o, who] = product(HA[who, lines, :], pair(QA, zq))

            @pl.when(c != h)
            def _():
                helper_core(o, who).start()

        each(low, high, body)

    def help_add_up(who, h, low, high):
        def body(o):
            helper_core(o, who).wait_recv()
            encode(HS.at[o, who], HSUM[0, o, who] + HCR[o, who])
            give_back(o, who).start()

        @pl.when(c == h)
        def _():
            each(low, high, body)

    total = 4 * (nz - 2)
    first = jnp.where(is_end, total, total - 2)
    early = jnp.where(is_end, nz - 1, 0)
    lax.fori_loop(0, first, relay, 0)

    @pl.when(is_helper)
    def _():
        for h in range(2):
            lend(1, h).wait_recv()
            help_multiply(1, h, 0, nz - 2)
            help_add_up(1, h, 0, nz - 2)

    @pl.when(~is_end)
    def _():
        for h in range(2):
            xd(h, 0).wait_recv()

    lax.fori_loop(first, jnp.maximum(first, total - 1), relay, 0)
    xd(0, 1).wait_recv()
    multiply(1, 0, 0, nz - 1)
    add_up(1, 0, 0, nz - 1)
    for h in range(2):
        multiply(0, h, 0, early)

    @pl.when(is_helper)
    def _():
        lend(0, 0).wait_recv()
        help_multiply(0, 0, 0, nz - 2)
        help_add_up(0, 0, 0, nz - 2)

    lax.fori_loop(jnp.maximum(first, total - 1), total, relay, 0)

    @pl.when(is_helper)
    def _():
        for h in range(2):
            help_multiply(1, h, nz - 2, nz - 1)
        help_multiply(0, 0, nz - 2, nz - 1)
        for h in range(2):
            help_add_up(1, h, nz - 2, nz - 1)
        help_add_up(0, 0, nz - 2, nz - 1)

    xd(1, 1).wait_recv()
    multiply(1, 1, 0, nz - 1)
    add_up(1, 1, 0, nz - 1)

    @pl.when(z == 0)
    def _():
        for h in range(4):
            from_above(total + h, 1).wait_recv()

    @pl.when(z == nz - 1)
    def _():
        for h in range(4):
            from_below(total + h, 1).wait_recv()

    for h in range(2):
        multiply(1, h, nz - 1, nz)

    @pl.when(is_helper)
    def _():
        lend(0, 1).wait_recv()
        help_multiply(0, 1, 0, nz - 1)

    for h in range(2):
        add_up(1, h, nz - 1, nz)

    @pl.when(is_helper)
    def _():
        help_add_up(0, 1, 0, nz - 1)

    for h in range(2):
        multiply(0, h, early, nz)
    for h in range(2):
        add_up(0, h, 0, nz)

    def finish(o):
        out(o).wait_recv()
        sums = decode(XR.at[o])
        for s in (0, 1):
            at = pl.multiple_of((z_of(o) * 2 + jnp.where(x == s, 0, 1)) * rows, rows)
            mine, theirs = pl.ds(s * rows, rows), slice((1 - s) * rows, (2 - s) * rows)
            o_ref[:, pl.ds(at, rows)] = SUM[0, o, 0, :, mine] + sums[:, theirs]

    each(0, nz, finish)

    for h in range(2):
        for part in (0, 1):
            xq(h, part).wait_send()
            xd(h, part).wait_send()

    for h in range(2):

        @pl.when(c != h)
        def _():
            each(0, nz, lambda o: [core(o, who).wait_send() for who in (0, 1)])

    each(0, nz, lambda o: out(o).wait_send())

    @pl.when(is_end)
    def _():
        for who in (0, 1):
            for h in range(2):
                lend(who, h).wait_send()

    @pl.when(is_helper)
    def _():
        def drain_help(o):
            for who in (0, 1):
                helper_core(o, who).wait_send()
                give_back(o, who).wait_send()

        each(0, nz - 1, drain_help)

    def drain_up(i, _):
        both_parts(lambda part: going_up(i, part).wait_send(), True, z < nz - 2)
        return 0

    def drain_down(i, _):
        both_parts(lambda part: going_down(i, part).wait_send(), True, z > 1)
        return 0

    @pl.when(has_above)
    def _():
        lax.fori_loop(0, 4 * (z + 1), drain_up, 0)

    @pl.when(has_below)
    def _():
        lax.fori_loop(0, 4 * (nz - z), drain_down, 0)


def exchange(queries, documents, n):
    rows, k = queries.shape
    nd = documents.shape[0] // 2
    nz, half = n // 2, k // 2
    ka = half // 128 * 3 // 8 * 128
    kb = half - ka
    block, coded = (nd, 2 * rows), (nd + 16, 2 * rows)
    dma = pltpu.SemaphoreType.DMA
    return pl.pallas_call(
        functools.partial(kernel, nz),
        out_shape=jax.ShapeDtypeStruct((nd, n * rows), jnp.float32),
        in_specs=[pl.BlockSpec(memory_space=pltpu.HBM)] * 2,
        out_specs=pl.BlockSpec(memory_space=pltpu.VMEM),
        scratch_shapes=[
            pltpu.VMEM((nz, 2, rows, ka), jnp.bfloat16),
            pltpu.VMEM((nz, 2, rows, kb), jnp.bfloat16),
            pltpu.VMEM((2, 2 * nd, ka), jnp.bfloat16),
            pltpu.VMEM((2, 2 * nd, kb), jnp.bfloat16),
            pltpu.VMEM((2, 2 * nd, ka), jnp.bfloat16),
            pltpu.VMEM((2, nz, 2) + block, jnp.float32),
            pltpu.VMEM((nz, 2) + block, jnp.float32),
            pltpu.VMEM((nz,) + coded, jnp.int16),
            pltpu.VMEM((nz,) + coded, jnp.int16),
            pltpu.VMEM((2, nz - 1, 2) + block, jnp.float32),
            pltpu.VMEM((nz - 1, 2) + block, jnp.float32),
            pltpu.VMEM((nz - 1, 2) + coded, jnp.int16),
            pltpu.VMEM((nz - 1, 2) + coded, jnp.int16),
            dma((4,)),
            dma((2, 2)), dma((2, 2)), dma((2, 2)), dma((2, 2)),
            dma((4 * nz, 2)), dma((4 * nz, 2)), dma((4 * nz, 2)), dma((4 * nz, 2)),
            dma((2, 2)), dma((2, 2)),
            dma((nz, 2)), dma((nz, 2)), dma((nz,)), dma((nz,)),
            dma((nz - 1, 2)), dma((nz - 1, 2)), dma((nz - 1, 2)), dma((nz - 1, 2)),
        ],
        compiler_params=pltpu.CompilerParams(
            collective_id=0, has_side_effects=True, vmem_limit_bytes=52 * 2**20
        ),
        cost_estimate=pl.CostEstimate(
            flops=4 * n * rows * nd * k, bytes_accessed=32 * 2**20, transcendentals=0
        ),
    )(queries, documents)


def on_device(n, query_grads, doc_grads, query_ids, doc_ids):
    queries = query_grads.reshape(query_grads.shape[0], -1)
    documents = doc_grads.reshape(doc_grads.shape[0], -1)
    rows, nd = queries.shape[0], documents.shape[0] // 2
    if rows % 128 or nd % 16 or n % 2 or n < 8 or n * rows > 1024 or queries.shape[1] % 2048:
        every = lax.all_gather(queries, "doc", axis=0, tiled=True)
        raw = lax.dot_general(every, documents, NT, preferred_element_type=jnp.float32)
        same = query_ids[:, None] == doc_ids[None, :]
        partial_scores = jnp.where(same, jnp.zeros_like(raw), raw)
        return lax.psum_scatter(partial_scores, "layer", scatter_dimension=1, tiled=True)
    raw = exchange(queries, documents, n)
    ids = jnp.where(lax.axis_index("layer") == 0, doc_ids[:nd], doc_ids[nd:])
    return jnp.where(ids[:, None] == query_ids[None, :], jnp.zeros_like(raw), raw).T


def solution(mesh):
    in_specs = (
        P(("grp", "doc"), "layer", None),
        P(("grp", "doc"), "layer", None),
        P("grp"),
        P(("grp", "doc")),
    )
    out_specs = P("grp", ("doc", "layer"))
    return jax.shard_map(
        functools.partial(on_device, mesh.shape["doc"]),
        mesh=mesh, in_specs=in_specs, out_specs=out_specs, check_vma=False,
    )
```

```python
import functools
import math

import jax
import jax.numpy as jnp
from jax import lax
from jax.experimental import pallas as pl
from jax.experimental.pallas import tpu as pltpu
from jax.sharding import PartitionSpec as P

MESH = pl.DeviceIdType.MESH
NT = (((1,), (1,)), ((), ()))
STEP = math.log(2) / 128
TOP = 32700.0


def encode(into, sums):
    n = sums.shape[0]
    peak = jnp.maximum(jnp.max(jnp.abs(sums), axis=0, keepdims=True), 1e-30)
    level = jnp.ceil(jnp.log(peak) / STEP) + 1
    units = jnp.round(sums * (jnp.exp(level * -STEP) * TOP))
    into[pl.ds(0, n)] = units.astype(jnp.int32).astype(jnp.int16)
    level = jnp.broadcast_to(level.astype(jnp.int32), (16, sums.shape[1]))
    into[pl.ds(n, 16)] = level.astype(jnp.int16)


def decode(coded):
    n = coded.shape[0] - 16
    level = coded[pl.ds(n, 16)].astype(jnp.int32).astype(jnp.float32)[:1]
    units = coded[pl.ds(0, n)].astype(jnp.int32).astype(jnp.float32)
    return units * (jnp.exp(level * STEP) / TOP)


def kernel(
    nz, q_ref, d_ref, o_ref, QA, QB, DA, DB, HA, SUM, CR, XS, XR, HSUM, HCR, HS, RET,
    loc, xq_s, xq_r, xd_s, xd_r, up_s, up_r, dn_s, dn_r, h_s, h_r, c_s, c_r, o_s, o_r, hc_s, hc_r, ret_s, ret_r,
):
    g, d, c = lax.axis_index("grp"), lax.axis_index("doc"), lax.axis_index("layer")
    z, x = d // 2, d % 2
    partner, other = (g, d + 1 - 2 * x, c), (g, d, 1 - c)
    above, below = (g, d + 2, c), (g, d - 2, c)
    has_above, has_below = z < nz - 1, z > 0
    is_end = (z == 0) | (z == nz - 1)
    is_helper = (z == 1) | (z == nz - 2)
    helper = (g, jnp.where(z == 0, d + 2, d - 2), c)
    helped = (g, jnp.where(z == 1, d - 2, d + 2), c)
    rows, ka, kb = QA.shape[2], QA.shape[3], QB.shape[3]
    half = ka + kb
    ch = rows // 2
    nd = DA.shape[1] // 2

    def columns(part, mine):
        start = jnp.where(mine, x, 1 - x) * half + (ka if part else 0)
        return pl.ds(pl.multiple_of(start, 128), kb if part else ka)

    barrier = pltpu.get_barrier_semaphore()

    def greet(device):
        pl.semaphore_signal(barrier, inc=1, device_id=device, device_id_type=MESH)

    greet(partner)
    greet(other)

    @pl.when(has_above)
    def _():
        greet(above)

    @pl.when(has_below)
    def _():
        greet(below)

    def own(part):
        Q, D = (QA, QB)[part], (DA, DB)[part]
        return (
            pltpu.make_async_copy(q_ref.at[:, columns(part, True)], Q.at[z, 0], loc.at[part]),
            pltpu.make_async_copy(d_ref.at[:, columns(part, True)], D.at[0], loc.at[2 + part]),
        )

    for part in (0, 1):
        for copy in own(part):
            copy.start()
    pl.semaphore_wait(barrier, 2 + jnp.where(has_above, 1, 0) + jnp.where(has_below, 1, 0))

    def remote(src, dst, ss, rs, device):
        return pltpu.make_async_remote_copy(
            src_ref=src, dst_ref=dst, send_sem=ss, recv_sem=rs, device_id=device, device_id_type=MESH
        )

    def xq(h, part):
        r = pl.ds(h * ch, ch)
        return remote(
            q_ref.at[r, columns(part, False)], (QA, QB)[part].at[z, 1, r], xq_s.at[h, part], xq_r.at[h, part], partner
        )

    def xd(h, part):
        r = pl.ds(h * nd, nd)
        return remote(
            d_ref.at[r, columns(part, False)], (DA, DB)[part].at[1, r], xd_s.at[h, part], xd_r.at[h, part], partner
        )

    def chunk(part, zq, sub):
        return (QA, QB)[part].at[zq, sub // 2, pl.ds(pl.multiple_of(sub % 2 * ch, ch), ch)]

    def going_up(i, part, first=False):
        at = chunk(part, z - i // 4, i % 4)
        src = q_ref.at[pl.ds(i * ch, ch), columns(part, True)] if first else at
        return remote(src, at, up_s.at[i, part], up_r.at[i, part], above)

    def going_down(i, part, first=False):
        at = chunk(part, z + i // 4, i % 4)
        src = q_ref.at[pl.ds(i * ch, ch), columns(part, True)] if first else at
        return remote(src, at, dn_s.at[i, part], dn_r.at[i, part], below)

    def from_below(i, part):
        at = chunk(part, z - 1 - i // 4, i % 4)
        return remote(at, at, up_s.at[i, part], up_r.at[i, part], above)

    def from_above(i, part):
        at = chunk(part, z + 1 + i // 4, i % 4)
        return remote(at, at, dn_s.at[i, part], dn_r.at[i, part], below)

    def both_parts(act, with_b, with_a):
        @pl.when(with_b)
        def _():
            act(1)

        @pl.when(with_a)
        def _():
            act(0)

    def send_up(i):
        both_parts(lambda part: going_up(i, part).start(), has_above, z < nz - 2)

    def send_down(i):
        both_parts(lambda part: going_down(i, part).start(), has_below, z > 1)

    for h in range(2):
        for part in (1, 0):
            xq(h, part).start()
    for h in range(2):
        both_parts(lambda part: going_up(h, part, True).start(), has_above, z < nz - 2)
        both_parts(lambda part: going_down(h, part, True).start(), has_below, z > 1)
    for h in range(2):
        for part in (1, 0):
            xq(h, part).wait_recv()
        send_up(2 + h)
        send_down(2 + h)
    for part in (0, 1):
        for h in range(2):
            xd(h, part).start()
    for part in (0, 1):
        for copy in own(part):
            copy.wait()

    def lend(who, h):
        at = pl.ds(h * nd, nd)
        return remote(DA.at[who, at], HA.at[who, at], h_s.at[who, h], h_r.at[who, h], helper)

    @pl.when(is_end)
    def _():
        for h in range(2):
            xd(h, 0).wait_recv()
            lend(1, h).start()
        for h in range(2):
            lend(0, h).start()

    n_above, n_below = 4 * (nz - 1 - z), 4 * z

    def relay(j, _):
        @pl.when(j < n_above)
        def _():
            both_parts(lambda part: from_above(j, part).wait_recv(), True, has_below)
            send_down(j + 4)

        @pl.when(j < n_below)
        def _():
            both_parts(lambda part: from_below(j, part).wait_recv(), True, has_above)
            send_up(j + 4)

        return 0

    def core(o, who):
        return remote(SUM.at[1, o, who], CR.at[o, who], c_s.at[o, who], c_r.at[o, who], other)

    def helper_core(o, who):
        return remote(HSUM.at[1, o, who], HCR.at[o, who], hc_s.at[o, who], hc_r.at[o, who], other)

    def give_back(o, who):
        return remote(HS.at[o, who], RET.at[o, who], ret_s.at[o, who], ret_r.at[o, who], helped)

    def out(o):
        return remote(XS.at[o], XR.at[o], o_s.at[o], o_r.at[o], partner)

    def z_of(o):
        return jnp.where(z < nz // 2, o, nz - 1 - o)

    def product(documents, queries):
        return lax.dot_general(documents, queries, NT, preferred_element_type=jnp.float32)

    def pair(ref, zq):
        return ref[zq].reshape(2 * rows, ref.shape[3])

    def each(low, high, body):
        lax.fori_loop(low, high, lambda o, _: (body(o), 0)[1], 0)

    def multiply(who, h, low, high):
        lines, slot = pl.ds(h * nd, nd), jnp.where(c == h, 0, 1)

        def body(o):
            zq = z_of(o)
            SUM[slot, o, who] = product(DB[who, lines, :], pair(QB, zq))

            @pl.when((~is_end) | (o == 0))
            def _():
                SUM[slot, o, who] = SUM[slot, o, who] + product(DA[who, lines, :], pair(QA, zq))

            @pl.when(c != h)
            def _():
                core(o, who).start()

        each(low, high, body)

    def add_up(who, h, low, high):
        def body(o):
            core(o, who).wait_recv()
            SUM[0, o, who] = SUM[0, o, who] + CR[o, who]

            @pl.when(is_end & (o > 0))
            def _():
                give_back(o - 1, who).wait_recv()
                SUM[0, o, who] = SUM[0, o, who] + decode(RET.at[o - 1, who])

            if who == 1:
                encode(XS.at[o], SUM[0, o, 1])
                out(o).start()

        @pl.when(c == h)
        def _():
            each(low, high, body)

    def help_multiply(who, h, low, high):
        lines, slot = pl.ds(h * nd, nd), jnp.where(c == h, 0, 1)

        def body(o):
            zq = jnp.where(z == 1, 1 + o, nz - 2 - o)
            HSUM[slot, o, who] = product(HA[who, lines, :], pair(QA, zq))

            @pl.when(c != h)
            def _():
                helper_core(o, who).start()

        each(low, high, body)

    def help_add_up(who, h, low, high):
        def body(o):
            helper_core(o, who).wait_recv()
            encode(HS.at[o, who], HSUM[0, o, who] + HCR[o, who])
            give_back(o, who).start()

        @pl.when(c == h)
        def _():
            each(low, high, body)

    total = 4 * (nz - 2)
    first = jnp.where(is_end, total, total - 2)
    early = jnp.where(is_end, nz - 1, 0)
    lax.fori_loop(0, first, relay, 0)

    @pl.when(is_helper)
    def _():
        for h in range(2):
            lend(1, h).wait_recv()
            help_multiply(1, h, 0, nz - 2)
            help_add_up(1, h, 0, nz - 2)

    @pl.when(~is_end)
    def _():
        for h in range(2):
            xd(h, 0).wait_recv()

    lax.fori_loop(first, jnp.maximum(first, total - 1), relay, 0)
    xd(0, 1).wait_recv()
    multiply(1, 0, 0, nz - 1)
    add_up(1, 0, 0, nz - 1)
    for h in range(2):
        multiply(0, h, 0, early)

    @pl.when(is_helper)
    def _():
        lend(0, 0).wait_recv()
        help_multiply(0, 0, 0, nz - 2)
        help_add_up(0, 0, 0, nz - 2)

    lax.fori_loop(jnp.maximum(first, total - 1), total, relay, 0)

    @pl.when(is_helper)
    def _():
        for h in range(2):
            help_multiply(1, h, nz - 2, nz - 1)
        help_multiply(0, 0, nz - 2, nz - 1)
        for h in range(2):
            help_add_up(1, h, nz - 2, nz - 1)
        help_add_up(0, 0, nz - 2, nz - 1)

    xd(1, 1).wait_recv()
    multiply(1, 1, 0, nz - 1)
    add_up(1, 1, 0, nz - 1)

    @pl.when(z == 0)
    def _():
        for h in range(4):
            from_above(total + h, 1).wait_recv()

    @pl.when(z == nz - 1)
    def _():
        for h in range(4):
            from_below(total + h, 1).wait_recv()

    for h in range(2):
        multiply(1, h, nz - 1, nz)

    @pl.when(is_helper)
    def _():
        lend(0, 1).wait_recv()
        help_multiply(0, 1, 0, nz - 1)

    for h in range(2):
        add_up(1, h, nz - 1, nz)

    @pl.when(is_helper)
    def _():
        help_add_up(0, 1, 0, nz - 1)

    for h in range(2):
        multiply(0, h, early, nz)
    for h in range(2):
        add_up(0, h, 0, nz)

    def finish(o):
        out(o).wait_recv()
        sums = decode(XR.at[o])
        for s in (0, 1):
            at = pl.multiple_of((z_of(o) * 2 + jnp.where(x == s, 0, 1)) * rows, rows)
            mine, theirs = pl.ds(s * rows, rows), slice((1 - s) * rows, (2 - s) * rows)
            o_ref[:, pl.ds(at, rows)] = SUM[0, o, 0, :, mine] + sums[:, theirs]

    each(0, nz, finish)

    for h in range(2):
        for part in (0, 1):
            xq(h, part).wait_send()
            xd(h, part).wait_send()

    for h in range(2):

        @pl.when(c != h)
        def _():
            each(0, nz, lambda o: [core(o, who).wait_send() for who in (0, 1)])

    each(0, nz, lambda o: out(o).wait_send())

    @pl.when(is_end)
    def _():
        for who in (0, 1):
            for h in range(2):
                lend(who, h).wait_send()

    @pl.when(is_helper)
    def _():
        def drain_help(o):
            for who in (0, 1):
                helper_core(o, who).wait_send()
                give_back(o, who).wait_send()

        each(0, nz - 1, drain_help)

    def drain_up(i, _):
        both_parts(lambda part: going_up(i, part).wait_send(), True, z < nz - 2)
        return 0

    def drain_down(i, _):
        both_parts(lambda part: going_down(i, part).wait_send(), True, z > 1)
        return 0

    @pl.when(has_above)
    def _():
        lax.fori_loop(0, 4 * (z + 1), drain_up, 0)

    @pl.when(has_below)
    def _():
        lax.fori_loop(0, 4 * (nz - z), drain_down, 0)


def exchange(queries, documents, n):
    rows, k = queries.shape
    nd = documents.shape[0] // 2
    nz, half = n // 2, k // 2
    ka = half // 128 * 7 // 16 * 128
    kb = half - ka
    block, coded = (nd, 2 * rows), (nd + 16, 2 * rows)
    dma = pltpu.SemaphoreType.DMA
    return pl.pallas_call(
        functools.partial(kernel, nz),
        out_shape=jax.ShapeDtypeStruct((nd, n * rows), jnp.float32),
        in_specs=[pl.BlockSpec(memory_space=pltpu.HBM)] * 2,
        out_specs=pl.BlockSpec(memory_space=pltpu.VMEM),
        scratch_shapes=[
            pltpu.VMEM((nz, 2, rows, ka), jnp.bfloat16),
            pltpu.VMEM((nz, 2, rows, kb), jnp.bfloat16),
            pltpu.VMEM((2, 2 * nd, ka), jnp.bfloat16),
            pltpu.VMEM((2, 2 * nd, kb), jnp.bfloat16),
            pltpu.VMEM((2, 2 * nd, ka), jnp.bfloat16),
            pltpu.VMEM((2, nz, 2) + block, jnp.float32),
            pltpu.VMEM((nz, 2) + block, jnp.float32),
            pltpu.VMEM((nz,) + coded, jnp.int16),
            pltpu.VMEM((nz,) + coded, jnp.int16),
            pltpu.VMEM((2, nz - 1, 2) + block, jnp.float32),
            pltpu.VMEM((nz - 1, 2) + block, jnp.float32),
            pltpu.VMEM((nz - 1, 2) + coded, jnp.int16),
            pltpu.VMEM((nz - 1, 2) + coded, jnp.int16),
            dma((4,)),
            dma((2, 2)), dma((2, 2)), dma((2, 2)), dma((2, 2)),
            dma((4 * nz, 2)), dma((4 * nz, 2)), dma((4 * nz, 2)), dma((4 * nz, 2)),
            dma((2, 2)), dma((2, 2)),
            dma((nz, 2)), dma((nz, 2)), dma((nz,)), dma((nz,)),
            dma((nz - 1, 2)), dma((nz - 1, 2)), dma((nz - 1, 2)), dma((nz - 1, 2)),
        ],
        compiler_params=pltpu.CompilerParams(
            collective_id=0, has_side_effects=True, vmem_limit_bytes=52 * 2**20
        ),
        cost_estimate=pl.CostEstimate(
            flops=4 * n * rows * nd * k, bytes_accessed=32 * 2**20, transcendentals=0
        ),
    )(queries, documents)


def on_device(n, query_grads, doc_grads, query_ids, doc_ids):
    queries = query_grads.reshape(query_grads.shape[0], -1)
    documents = doc_grads.reshape(doc_grads.shape[0], -1)
    rows, nd = queries.shape[0], documents.shape[0] // 2
    if rows % 128 or nd % 16 or n % 2 or n < 8 or n * rows > 1024 or queries.shape[1] % 2048:
        every = lax.all_gather(queries, "doc", axis=0, tiled=True)
        raw = lax.dot_general(every, documents, NT, preferred_element_type=jnp.float32)
        same = query_ids[:, None] == doc_ids[None, :]
        partial_scores = jnp.where(same, jnp.zeros_like(raw), raw)
        return lax.psum_scatter(partial_scores, "layer", scatter_dimension=1, tiled=True)
    raw = exchange(queries, documents, n)
    ids = jnp.where(lax.axis_index("layer") == 0, doc_ids[:nd], doc_ids[nd:])
    return jnp.where(ids[:, None] == query_ids[None, :], jnp.zeros_like(raw), raw).T


def solution(mesh):
    in_specs = (
        P(("grp", "doc"), "layer", None),
        P(("grp", "doc"), "layer", None),
        P("grp"),
        P(("grp", "doc")),
    )
    out_specs = P("grp", ("doc", "layer"))
    return jax.shard_map(
        functools.partial(on_device, mesh.shape["doc"]),
        mesh=mesh, in_specs=in_specs, out_specs=out_specs, check_vma=False,
    )
```
